32 devices in a mesh: dp: 16 (over z, y, x), shard: 2 (over core).
Axes of the slice: x: 2, y: 2, z: 4, core: 2. Of those that a mesh axis runs over, the one named last changes fastest.
Arguments:
- activations: bfloat16 [16384, 1984], P('dp'), may hold values from -6 to 6
- out_grads: bfloat16 [16384, 1984], P('dp', 'shard'), may hold values from -1.1953125 to 1.1953125
- error_state: bfloat16 [31744, 1984], P('dp', 'shard'), may hold values from -4 to 4
- basis: float32 [1984, 128], P('shard'), may hold values from -0.125 to 0.125
- master: float32 [1984, 1984], P('dp', 'shard'), may hold values from -0.125 to 0.125
- first_moment: float32 [1984, 1984], P('dp', 'shard'), may hold values from -0.3 to 0.3
- second_moment: float32 [1984, 1984], P('dp', 'shard'), may hold values from 0.0001 to 0.01
Outputs:
- new_params: bfloat16 [1984, 1984], P('dp')
- new_error: bfloat16 [31744, 1984], P('dp', 'shard')
- update: float32 [1984, 1984], P('dp', 'shard')
- new_first: float32 [1984, 1984], P('dp', 'shard')
- new_second: float32 [1984, 1984], P('dp', 'shard')
- new_master: float32 [1984, 1984], P('dp', 'shard')
- new_basis: float32 [1984, 128], P('shard')
The draws below stay inside these ranges and needn't reach their ends.
All inputs are finite; a program needn't handle non-finite values.
Results may differ from the reference program's by a relative error of at most 0.0004.
Values may be sent and summed in bfloat16 or wider, within the bound.
A program may use at most 128 MiB of HBM per device.

```python
import math
import jax
import jax.numpy as jnp
from jax import lax

ROWS = 1984
COLS = 1984
RANK = 128
TOK_DEV = 1024
TOKENS = 16384
REPLICA_ROWS = 31744
N_DP = 16


def levels(stream_key, dims, shards, least, high):
    def one(dim, parts):
        steps = jax.random.uniform(jax.random.fold_in(jax.random.fold_in(stream_key, 6), dim), (parts,), jnp.float32, least / len(shards), high / len(shards))
        return jnp.repeat(jnp.exp(steps), dims[dim] // parts).reshape((-1,) + (1,) * (len(dims) - dim - 1))

    gain = one(*shards[0])
    for cut in shards[1:]:
        gain = gain * one(*cut)
    return gain


def gaussian(rng, dims, scale, reach, split=(), kind=jnp.bfloat16):
    entries = jax.random.normal(rng, dims, jnp.float32) * scale
    if len(split) > 0:
        entries = levels(rng, dims, split, -0.22, 0.18) * entries
    return jnp.clip(entries, min=-reach, max=reach).astype(kind)


def setup_inputs(seed: int = 0) -> dict:
    streams_of = jax.random.split(jax.random.key(seed), 8)
    return {
        "activations": gaussian(streams_of[0], (TOKENS, ROWS), 1.0, 6.0, ((0, 16),)),
        "out_grads": gaussian(streams_of[1], (TOKENS, COLS), 0.18, 1.1953125, ((0, 16), (1, 2))),
        "error_state": gaussian(streams_of[2], (REPLICA_ROWS, COLS), 0.5, 4.0, ((0, 16), (1, 2))),
        "basis": gaussian(streams_of[3], (COLS, RANK), COLS ** -0.5, 0.125, ((0, 2),), jnp.float32),
        "master": gaussian(streams_of[4], (ROWS, COLS), ROWS ** -0.5, 0.125, ((0, 16), (1, 2)), jnp.float32),
        "first_moment": gaussian(streams_of[5], (ROWS, COLS), 0.05, 0.3, ((0, 16), (1, 2)), jnp.float32),
        "second_moment": jnp.clip(jnp.exp(math.log(0.01) - 4.6051702 * jax.random.uniform(streams_of[6], (ROWS, COLS), jnp.float32) ** levels(streams_of[6], (ROWS, COLS), ((0, 16), (1, 2)), -0.2, 0.2)), 0.0001, 0.01),
    }


beta_one = 0.9
beta_two = 0.95
step_size = 0.001
adam_epsilon = 1e-08
ridge_scale = 1e-06
highest = lax.Precision.HIGHEST

def orthonormalize(summed):
    gram_matrix = jnp.dot(summed.T, summed, precision=highest)
    width = gram_matrix.shape[0]
    ridge_term = ridge_scale * jnp.trace(gram_matrix) / width * jnp.eye(width, dtype=gram_matrix.dtype)
    factor = jnp.linalg.cholesky(gram_matrix + ridge_term)
    return jax.scipy.linalg.solve_triangular(factor, summed.T, lower=True).T

def reference(activations, out_grads, error_state, basis, master, first_moment, second_moment):
    act_blocks = activations.reshape(N_DP, TOK_DEV, ROWS)
    grad_blocks = out_grads.reshape(N_DP, TOK_DEV, COLS)
    error_blocks = error_state.reshape(N_DP, ROWS, COLS)

    def merge_replica(operands):
        act_rows, grad_rows, error_rows = operands
        product = lax.dot_general(act_rows.astype(jnp.float32), grad_rows.astype(jnp.float32), (((0,), (0,)), ((), ())), preferred_element_type=jnp.float32)
        return product + error_rows.astype(jnp.float32)
    merged = lax.map(merge_replica, (act_blocks, grad_blocks, error_blocks))

    def add_left(running, matrix):
        return (running + jnp.dot(matrix, basis, precision=highest), None)
    summed, unused = lax.scan(add_left, jnp.zeros((ROWS, RANK), jnp.float32), merged)
    orthonormal = orthonormalize(summed)

    def add_right(running, matrix):
        term = lax.dot_general(matrix, orthonormal, (((0,), (0,)), ((), ())), precision=highest)
        return (running + term, None)
    total_right, unused = lax.scan(add_right, jnp.zeros((COLS, RANK), jnp.float32), merged)
    new_basis = total_right / N_DP
    update = lax.dot_general(orthonormal, new_basis, (((1,), (1,)), ((), ())), precision=highest)
    new_error = (merged - update[None]).astype(jnp.bfloat16).reshape(N_DP * ROWS, COLS)
    new_first = beta_one * first_moment + (1.0 - beta_one) * update
    new_second = beta_two * second_moment + (1.0 - beta_two) * update * update
    new_master = master - step_size * new_first / (jnp.sqrt(new_second) + adam_epsilon)
    new_params = new_master.astype(jnp.bfloat16)
    return (new_params, new_error, update, new_first, new_second, new_master, new_basis)
```

```python
import functools

import jax
import jax.numpy as jnp
from jax import lax
from jax.experimental import pallas as pl
from jax.experimental.pallas import tpu as pltpu
from jax.sharding import PartitionSpec as P

beta_one = 0.9
beta_two = 0.95
step_size = 0.001
adam_epsilon = 1e-08
ridge_scale = 1e-06
highest = lax.Precision.HIGHEST
high = lax.Precision.HIGH
MESH = pl.DeviceIdType.MESH


def solve_rows(gram_matrix, row_piece):
    width = gram_matrix.shape[0]
    ridge_term = (
        ridge_scale * jnp.trace(gram_matrix) / width * jnp.eye(width, dtype=gram_matrix.dtype)
    )
    factor = jnp.linalg.cholesky(gram_matrix + ridge_term)
    return jax.scipy.linalg.solve_triangular(factor, row_piece.T, lower=True).T


def adam(update, master, first_moment, second_moment):
    new_first = beta_one * first_moment + (1.0 - beta_one) * update
    new_second = beta_two * second_moment + (1.0 - beta_two) * update * update
    new_master = master - step_size * new_first / (jnp.sqrt(new_second) + adam_epsilon)
    return new_first, new_second, new_master


def rows_at(index, size):
    return pl.ds(pl.multiple_of(index * size, size), size)


def greet(minor, major, pair):
    dp, core = lax.axis_index("dp"), lax.axis_index("shard")
    q, z = lax.rem(dp, minor), lax.div(dp, minor)
    barrier = pltpu.get_barrier_semaphore()
    count = 0
    if pair:
        pl.semaphore_signal(
            barrier, inc=1, device_id={"dp": dp, "shard": 1 - core}, device_id_type=MESH
        )
        count += 1
    for j in range(1, minor):
        peer = z * minor + lax.rem(q + j, minor)
        pl.semaphore_signal(
            barrier, inc=1, device_id={"dp": peer, "shard": core}, device_id_type=MESH
        )
        count += 1
    for j in range(1, major):
        peer = lax.rem(z + j, major) * minor + q
        pl.semaphore_signal(
            barrier, inc=1, device_id={"dp": peer, "shard": core}, device_id_type=MESH
        )
        count += 1
    pl.semaphore_wait(barrier, count)


def push(src, dst, send, recv, slot, dp, core):
    copy = pltpu.make_async_remote_copy(
        src_ref=src,
        dst_ref=dst,
        send_sem=send.at[slot],
        recv_sem=recv.at[slot],
        device_id={"dp": dp, "shard": core},
        device_id_type=MESH,
    )
    copy.start()
    return copy


def scatter_minor(minor, source, land, send, recv, slot):
    dp, core = lax.axis_index("dp"), lax.axis_index("shard")
    q, z = lax.rem(dp, minor), lax.div(dp, minor)
    size = source.shape[0] // minor
    copies = []
    for j in range(1, minor):
        to = lax.rem(q + j, minor)
        copies.append(
            push(source.at[rows_at(to, size)], land.at[j - 1], send, recv, slot + j - 1,
                 z * minor + to, core)
        )
    return copies


def scatter_major(minor, major, source, land, send, recv, slot):
    dp, core = lax.axis_index("dp"), lax.axis_index("shard")
    q, z = lax.rem(dp, minor), lax.div(dp, minor)
    size = source.shape[0] // major
    copies = []
    for j in range(1, major):
        to = lax.rem(z + j, major)
        copies.append(
            push(source.at[rows_at(to, size)], land.at[j - 1], send, recv, slot + j - 1,
                 to * minor + q, core)
        )
    return copies


def gather(minor, major, along_major, ref, rows, send, recv, slot):
    dp, core = lax.axis_index("dp"), lax.axis_index("shard")
    q, z = lax.rem(dp, minor), lax.div(dp, minor)
    copies = []
    for j in range(1, major if along_major else minor):
        if along_major:
            peer = lax.rem(z + j, major) * minor + q
        else:
            peer = z * minor + lax.rem(q + j, minor)
        copies.append(push(ref.at[rows], ref.at[rows], send, recv, slot + j - 1, peer, core))
    return copies


def arrive(copies):
    for copy in copies:
        copy.wait()


def left_kernel(minor, major, part, total, half, quarter, land_core, land_minor, land_major,
                send, recv):
    dp, core = lax.axis_index("dp"), lax.axis_index("shard")
    q, z = lax.rem(dp, minor), lax.div(dp, minor)
    greet(minor, major, True)
    n_half = half.shape[0]
    n_quarter = quarter.shape[0]
    n_own = n_quarter // major
    arrive([push(part.at[rows_at(1 - core, n_half)], land_core, send, recv, 0, dp, 1 - core)])
    half[...] = part[rows_at(core, n_half), :] + land_core[...]
    arrive(scatter_minor(minor, half, land_minor, send, recv, 1))
    value = half[rows_at(q, n_quarter), :]
    for j in range(minor - 1):
        value = value + land_minor[j]
    quarter[...] = value
    slot = minor
    arrive(scatter_major(minor, major, quarter, land_major, send, recv, slot))
    slot += major - 1
    value = quarter[rows_at(z, n_own), :]
    for j in range(major - 1):
        value = value + land_major[j]
    own = rows_at((core * minor + q) * major + z, n_own)
    total[own, :] = value
    arrive(gather(minor, major, True, total, own, send, recv, slot))
    slot += major - 1
    own = rows_at(core * minor + q, n_quarter)
    arrive(gather(minor, major, False, total, own, send, recv, slot))
    slot += minor - 1
    own = rows_at(core, n_half)
    arrive([push(total.at[own], total.at[own], send, recv, slot, dp, 1 - core)])


def sum_left(part, minor, major):
    rows, rank = part.shape
    n_half = rows // 2
    n_quarter = n_half // minor
    n_own = n_quarter // major
    copies = 2 + 2 * (minor - 1) + 2 * (major - 1)
    vmem = pl.BlockSpec(memory_space=pltpu.VMEM)
    f32 = jnp.float32
    return pl.pallas_call(
        functools.partial(left_kernel, minor, major),
        out_shape=jax.ShapeDtypeStruct((rows, rank), f32),
        in_specs=[vmem],
        out_specs=vmem,
        scratch_shapes=[
            pltpu.VMEM((n_half, rank), f32),
            pltpu.VMEM((n_quarter, rank), f32),
            pltpu.VMEM((n_half, rank), f32),
            pltpu.VMEM((minor - 1, n_quarter, rank), f32),
            pltpu.VMEM((major - 1, n_own, rank), f32),
            pltpu.SemaphoreType.DMA((copies,)),
            pltpu.SemaphoreType.DMA((copies,)),
        ],
        compiler_params=pltpu.CompilerParams(
            collective_id=0, has_side_effects=True, vmem_limit_bytes=32 * 1024 * 1024
        ),
    )(part)


def invert_factor(gram, work):
    rank = gram.shape[0]
    lane = lax.broadcasted_iota(jnp.int32, (rank, rank), 1)
    line = lax.broadcasted_iota(jnp.int32, (rank, rank), 0)
    eye = lane == line
    trace = jnp.sum(jnp.where(eye, gram, 0.0), keepdims=True)
    work[:, :rank] = gram + jnp.where(eye, ridge_scale * trace / rank, 0.0)
    work[:, rank:] = jnp.where(eye, 1.0, 0.0)

    def step(j, carry):
        row = work[pl.ds(j, 1), :]
        left = work[:, :rank]
        column = jnp.sum(jnp.where(lane == j, left, 0.0), axis=1, keepdims=True)
        pivot = jnp.sum(
            jnp.where(lane[:1] == j, row[:, :rank], 0.0), axis=1, keepdims=True
        )
        scale = jnp.where(line[:, :1] > j, column / pivot, 0.0)
        work[...] = work[...] - scale * row
        return carry

    lax.fori_loop(0, rank, step, 0)
    pivots = jnp.sum(jnp.where(eye, work[:, :rank], 0.0), axis=1, keepdims=True)
    return work[:, rank:] * lax.rsqrt(pivots)


def right_kernel(minor, major, rows, part, left, basis, ortho, quarter, land_minor, land_major,
                 total, work, inverse, send, recv):
    dp = lax.axis_index("dp")
    q, z = lax.rem(dp, minor), lax.div(dp, minor)
    greet(minor, major, False)
    n_quarter = quarter.shape[0]
    n_own = n_quarter // major
    copies = scatter_minor(minor, part, land_minor, send, recv, 0)
    summed = left[...]
    gram = lax.dot_general(
        summed, summed, (((0,), (0,)), ((), ())), precision=highest,
        preferred_element_type=jnp.float32,
    )
    inverse[...] = invert_factor(gram, work)
    ortho[...] = lax.dot_general(
        left[:rows, :], inverse[...], (((1,), (1,)), ((), ())), precision=highest,
        preferred_element_type=jnp.float32,
    )
    arrive(copies)
    value = part[rows_at(q, n_quarter), :]
    for j in range(minor - 1):
        value = value + land_minor[j]
    quarter[...] = value
    slot = minor - 1
    arrive(scatter_major(minor, major, quarter, land_major, send, recv, slot))
    slot += major - 1
    value = quarter[rows_at(z, n_own), :]
    for j in range(major - 1):
        value = value + land_major[j]
    own = rows_at(q * major + z, n_own)
    total[own, :] = value
    arrive(gather(minor, major, True, total, own, send, recv, slot))
    slot += major - 1
    own = rows_at(q, n_quarter)
    arrive(gather(minor, major, False, total, own, send, recv, slot))
    basis[...] = lax.dot_general(
        inverse[...], total[...], (((1,), (0,)), ((), ())), precision=highest,
        preferred_element_type=jnp.float32,
    ) * (1.0 / (minor * major))


def sum_right(part, left, rows, minor, major):
    rank, columns = part.shape
    n_quarter = rank // minor
    n_own = n_quarter // major
    copies = 2 * (minor - 1) + 2 * (major - 1)
    vmem = pl.BlockSpec(memory_space=pltpu.VMEM)
    f32 = jnp.float32
    return pl.pallas_call(
        functools.partial(right_kernel, minor, major, rows),
        out_shape=(
            jax.ShapeDtypeStruct((rank, columns), f32),
            jax.ShapeDtypeStruct((rows, rank), f32),
        ),
        in_specs=[vmem, vmem],
        out_specs=(vmem, vmem),
        scratch_shapes=[
            pltpu.VMEM((n_quarter, columns), f32),
            pltpu.VMEM((minor - 1, n_quarter, columns), f32),
            pltpu.VMEM((major - 1, n_own, columns), f32),
            pltpu.VMEM((rank, columns), f32),
            pltpu.VMEM((rank, 2 * rank), f32),
            pltpu.VMEM((rank, rank), f32),
            pltpu.SemaphoreType.DMA((copies,)),
            pltpu.SemaphoreType.DMA((copies,)),
        ],
        compiler_params=pltpu.CompilerParams(
            collective_id=1, has_side_effects=True, vmem_limit_bytes=48 * 1024 * 1024
        ),
    )(part, left)


def pushed(minor, major, activations, out_grads, error_state, basis, master, first_moment,
           second_moment):
    product = lax.dot_general(
        activations, out_grads, (((0,), (0,)), ((), ())), preferred_element_type=jnp.float32
    )
    merged = product + error_state.astype(jnp.float32)
    rows = merged.shape[0]
    chunk = 16 * minor * major
    padded = -(-rows // chunk) * chunk
    part = jnp.dot(merged, basis, precision=high)
    left = sum_left(jnp.pad(part, ((0, padded - rows), (0, 0))), minor, major)
    right = lax.dot_general(left[:rows], merged, (((0,), (0,)), ((), ())), precision=high)
    basis_rows, orthonormal = sum_right(right, left, rows, minor, major)
    decompressed = jnp.dot(orthonormal, basis_rows, precision=high)
    new_error = (merged - decompressed).astype(jnp.bfloat16)
    rows_dev = master.shape[0]
    row_offset = lax.axis_index("dp") * rows_dev
    update = jnp.dot(
        lax.dynamic_slice_in_dim(orthonormal, row_offset, rows_dev, 0), basis_rows, precision=high
    )
    new_first, new_second, new_master = adam(update, master, first_moment, second_moment)
    new_params = lax.all_gather(new_master.astype(jnp.bfloat16), "shard", axis=1, tiled=True)
    return (new_params, new_error, update, new_first, new_second, new_master, basis_rows.T)


def summed_by_psum(activations, out_grads, error_state, basis, master, first_moment,
                   second_moment):
    product = lax.dot_general(
        activations, out_grads, (((0,), (0,)), ((), ())), preferred_element_type=jnp.float32
    )
    merged = product + error_state.astype(jnp.float32)
    rows_dev = master.shape[0]
    partial_value = jnp.dot(merged, basis, precision=highest)
    summed = lax.psum(partial_value, ("dp", "shard"))
    gram_matrix = jnp.dot(summed.T, summed, precision=highest)
    orthonormal = solve_rows(gram_matrix, summed)
    local_right = lax.dot_general(merged, orthonormal, (((0,), (0,)), ((), ())), precision=highest)
    new_basis = lax.psum(local_right, "dp") / lax.axis_size("dp")
    decompressed = lax.dot_general(
        orthonormal, new_basis, (((1,), (1,)), ((), ())), precision=highest
    )
    new_error = (merged - decompressed).astype(jnp.bfloat16)
    row_offset = lax.axis_index("dp") * rows_dev
    update = lax.dynamic_slice_in_dim(decompressed, row_offset, rows_dev, 0)
    new_first, new_second, new_master = adam(update, master, first_moment, second_moment)
    new_params = lax.all_gather(new_master.astype(jnp.bfloat16), "shard", axis=1, tiled=True)
    return (new_params, new_error, update, new_first, new_second, new_master, new_basis)


def solution(mesh):
    replicas, shards = mesh.shape["dp"], mesh.shape["shard"]
    minor = 1
    while minor * minor < replicas:
        minor *= 2
    major = replicas // minor
    placed = (
        P("dp", None),
        P("dp", "shard"),
        P("dp", "shard"),
        P("shard", None),
        P("dp", "shard"),
        P("dp", "shard"),
        P("dp", "shard"),
    )

    def step(activations, out_grads, error_state, basis, master, first_moment, second_moment):
        if shards == 2 and minor * major == replicas and basis.shape[1] % (8 * replicas) == 0:
            body = functools.partial(pushed, minor, major)
        else:
            body = summed_by_psum
        return jax.shard_map(
            body,
            mesh=mesh,
            in_specs=placed,
            out_specs=(
                P("dp", None),
                P("dp", "shard"),
                P("dp", "shard"),
                P("dp", "shard"),
                P("dp", "shard"),
                P("dp", "shard"),
                P("shard", None),
            ),
            check_vma=False,
        )(activations, out_grads, error_state, basis, master, first_moment, second_moment)

    return step
```

```python
import functools

import jax
import jax.numpy as jnp
from jax import lax
from jax.experimental import pallas as pl
from jax.experimental.pallas import tpu as pltpu
from jax.sharding import PartitionSpec as P

beta_one = 0.9
beta_two = 0.95
step_size = 0.001
adam_epsilon = 1e-08
ridge_scale = 1e-06
highest = lax.Precision.HIGHEST
high = lax.Precision.HIGH
MESH = pl.DeviceIdType.MESH


def solve_rows(gram_matrix, row_piece):
    width = gram_matrix.shape[0]
    ridge_term = (
        ridge_scale * jnp.trace(gram_matrix) / width * jnp.eye(width, dtype=gram_matrix.dtype)
    )
    factor = jnp.linalg.cholesky(gram_matrix + ridge_term)
    return jax.scipy.linalg.solve_triangular(factor, row_piece.T, lower=True).T


def adam(update, master, first_moment, second_moment):
    new_first = beta_one * first_moment + (1.0 - beta_one) * update
    new_second = beta_two * second_moment + (1.0 - beta_two) * update * update
    new_master = master - step_size * new_first / (jnp.sqrt(new_second) + adam_epsilon)
    return new_first, new_second, new_master


def rows_at(index, size):
    return pl.ds(pl.multiple_of(index * size, size), size)


def greet(minor, major, pair):
    dp, core = lax.axis_index("dp"), lax.axis_index("shard")
    q, z = lax.rem(dp, minor), lax.div(dp, minor)
    barrier = pltpu.get_barrier_semaphore()
    count = 0
    if pair:
        pl.semaphore_signal(
            barrier, inc=1, device_id={"dp": dp, "shard": 1 - core}, device_id_type=MESH
        )
        count += 1
    for j in range(1, minor):
        peer = z * minor + lax.rem(q + j, minor)
        pl.semaphore_signal(
            barrier, inc=1, device_id={"dp": peer, "shard": core}, device_id_type=MESH
        )
        count += 1
    for j in range(1, major):
        peer = lax.rem(z + j, major) * minor + q
        pl.semaphore_signal(
            barrier, inc=1, device_id={"dp": peer, "shard": core}, device_id_type=MESH
        )
        count += 1
    pl.semaphore_wait(barrier, count)


def push(src, dst, send, recv, slot, dp, core):
    copy = pltpu.make_async_remote_copy(
        src_ref=src,
        dst_ref=dst,
        send_sem=send.at[slot],
        recv_sem=recv.at[slot],
        device_id={"dp": dp, "shard": core},
        device_id_type=MESH,
    )
    copy.start()
    return copy


def scatter_minor(minor, source, land, send, recv, slot):
    dp, core = lax.axis_index("dp"), lax.axis_index("shard")
    q, z = lax.rem(dp, minor), lax.div(dp, minor)
    size = source.shape[0] // minor
    copies = []
    for j in range(1, minor):
        to = lax.rem(q + j, minor)
        copies.append(
            push(source.at[rows_at(to, size)], land.at[j - 1], send, recv, slot + j - 1,
                 z * minor + to, core)
        )
    return copies


def scatter_major(minor, major, source, land, send, recv, slot):
    dp, core = lax.axis_index("dp"), lax.axis_index("shard")
    q, z = lax.rem(dp, minor), lax.div(dp, minor)
    size = source.shape[0] // major
    copies = []
    for j in range(1, major):
        to = lax.rem(z + j, major)
        copies.append(
            push(source.at[rows_at(to, size)], land.at[j - 1], send, recv, slot + j - 1,
                 to * minor + q, core)
        )
    return copies


def gather(minor, major, along_major, ref, rows, send, recv, slot):
    dp, core = lax.axis_index("dp"), lax.axis_index("shard")
    q, z = lax.rem(dp, minor), lax.div(dp, minor)
    copies = []
    for j in range(1, major if along_major else minor):
        if along_major:
            peer = lax.rem(z + j, major) * minor + q
        else:
            peer = z * minor + lax.rem(q + j, minor)
        copies.append(push(ref.at[rows], ref.at[rows], send, recv, slot + j - 1, peer, core))
    return copies


def arrive(copies):
    for copy in copies:
        copy.wait()


def halves(value):
    top = value.astype(jnp.bfloat16)
    rest = (value - top.astype(jnp.float32)).astype(jnp.bfloat16)
    return jnp.concatenate([top, rest], axis=0)


def fold(value):
    rank = value.shape[0] // 2
    return value[:rank] + value[rank:]


def dot(left, right, left_dim, right_dim, precision=None):
    return lax.dot_general(
        left, right, (((left_dim,), (right_dim,)), ((), ())), precision=precision,
        preferred_element_type=jnp.float32,
    )


def begin_factor(gram, work):
    rank = gram.shape[0]
    lane = lax.broadcasted_iota(jnp.int32, (rank, rank), 1)
    line = lax.broadcasted_iota(jnp.int32, (rank, rank), 0)
    trace = jnp.sum(jnp.where(lane == line, gram, 0.0), keepdims=True)
    work[...] = gram + jnp.where(lane == line, ridge_scale * trace / rank, 0.0)


def eliminate(work, first, last):
    rank = work.shape[0]
    lane = lax.broadcasted_iota(jnp.int32, (rank, rank), 1)
    line = lax.broadcasted_iota(jnp.int32, (rank, rank), 0)
    lane_row, line_column = lane[:1], line[:, :1]

    def pick(value, index, places):
        return jnp.sum(jnp.where(places == index, value, 0.0), axis=1, keepdims=True)

    def step(pair, carry):
        j = 2 * pair
        k = j + 1
        matrix = work[...]
        row_j, row_k = work[pl.ds(j, 1), :], work[pl.ds(k, 1), :]
        column_j, column_k = pick(matrix, j, lane), pick(matrix, k, lane)
        jj, jk = pick(row_j, j, lane_row), pick(row_j, k, lane_row)
        kj, kk = pick(row_k, j, lane_row), pick(row_k, k, lane_row)
        inverse_j = 1.0 / jj
        ratio = kj * inverse_j
        inverse_k = 1.0 / (kk - ratio * jk)
        scale_j = jnp.where(line_column > j, column_j * inverse_j, 0.0)
        scale_k = jnp.where(line_column > k, (column_k - scale_j * jk) * inverse_k, 0.0)
        unit_j = jnp.where(lane_row == j, 1.0, row_j)
        unit_k = jnp.where(
            lane_row == k, 1.0, jnp.where(lane_row == j, 0.0, row_k) - ratio * unit_j
        )
        matrix = jnp.where((lane == j) & (line > j), 0.0, matrix) - scale_j * unit_j
        matrix = jnp.where((lane == k) & (line > k), 0.0, matrix) - scale_k * unit_k
        work[...] = matrix
        return carry

    lax.fori_loop(first, last, step, 0)


def finish_factor(work):
    rank = work.shape[0]
    lane = lax.broadcasted_iota(jnp.int32, (rank, rank), 1)
    line = lax.broadcasted_iota(jnp.int32, (rank, rank), 0)
    value = work[...]
    pivots = jnp.sum(jnp.where(lane == line, value, 0.0), axis=1, keepdims=True)
    unit = jnp.where(lane == line, 1.0, jnp.where(lane < line, value, 0.0))
    return unit * lax.rsqrt(pivots)


def factor_kernel(minor, major, a_far, b_far, e_far, basis, merged_far, ortho, new_basis,
                  a, b, e, merged, merged_top, merged_rest,
                  part, half, land_core, quarter, land_minor, land_major, total,
                  right, quarter_right, land_minor_right, land_major_right, total_right,
                  work, inverse, send, recv, local):
    dp, core = lax.axis_index("dp"), lax.axis_index("shard")
    q, z = lax.rem(dp, minor), lax.div(dp, minor)
    loads = [
        pltpu.make_async_copy(far, near, local.at[i])
        for i, (far, near) in enumerate(((b_far, b), (a_far, a), (e_far, e)))
    ]
    for load in loads:
        load.start()
    greet(minor, major, True)

    rows, columns = merged.shape
    width = half.shape[1]
    spans = [(0, width), (width, rows - width)]
    basis_parts = halves(basis[...].T)
    loads[0].wait()
    token_parts = halves(fold(dot(basis_parts, b[...], 1, 1)))
    loads[1].wait()
    loads[2].wait()
    for h, (start, size) in enumerate(spans):
        value = fold(
            dot(token_parts, a[:, start:start + size], 1, 0)
            + dot(basis_parts, e[start:start + size, :], 1, 1)
        )
        if size < width:
            part[h] = jnp.zeros_like(half)
        part[h, :, :size] = value

    def keep(place, value):
        merged[place, :] = value
        top = value.astype(jnp.bfloat16)
        merged_top[place, :] = top
        merged_rest[place, :] = (value - top.astype(jnp.float32)).astype(jnp.bfloat16)

    def tile(i, carry):
        place = rows_at(i, 256)
        keep(place, dot(a[:, place], b[...], 0, 0) + e[place, :].astype(jnp.float32))
        return carry

    full = rows // 256
    cuts = [min(cut, full) for cut in (0, 1, 4, 5, 6)] + [full]

    def tiles(stage):
        if cuts[stage] < cuts[stage + 1]:
            lax.fori_loop(cuts[stage], cuts[stage + 1], tile, 0)

    slot = 0
    copies = [push(part.at[1 - core], land_core, send, recv, slot, dp, 1 - core)]
    slot += 1
    tiles(0)
    arrive(copies)
    half[...] = part[core] + land_core[...]
    copies = scatter_minor(minor, half, land_minor, send, recv, slot)
    slot += minor - 1
    tiles(1)
    arrive(copies)
    n_quarter = quarter.shape[0]
    n_own = n_quarter // major
    value = half[rows_at(q, n_quarter), :]
    for j in range(minor - 1):
        value = value + land_minor[j]
    quarter[...] = value
    copies = scatter_major(minor, major, quarter, land_major, send, recv, slot)
    slot += major - 1
    tiles(2)
    arrive(copies)
    value = quarter[rows_at(z, n_own), :]
    for j in range(major - 1):
        value = value + land_major[j]
    mine = total.at[core]
    own = rows_at(q * major + z, n_own)
    mine[own, :] = value
    copies = gather(minor, major, True, mine, own, send, recv, slot)
    slot += major - 1
    tiles(3)
    arrive(copies)
    copies = gather(minor, major, False, mine, rows_at(q, n_quarter), send, recv, slot)
    slot += minor - 1
    tiles(4)
    if full * 256 < rows:
        place = slice(full * 256, rows)
        keep(place, dot(a[:, place], b[...], 0, 0) + e[place, :].astype(jnp.float32))
    store = pltpu.make_async_copy(merged, merged_far, local.at[3])
    store.start()
    arrive(copies)
    copy = push(mine, mine, send, recv, slot, dp, 1 - core)
    slot += 1
    copy.wait()

    rank = work.shape[0]
    for h, (start, size) in enumerate(spans):
        place = slice(start, start + size)
        parts = halves(total[h, :, :size])
        value = fold(dot(parts, merged_top[place, :], 1, 0)) + dot(
            parts[:rank], merged_rest[place, :], 1, 0
        )
        right[...] = value if h == 0 else right[...] + value
    copies = scatter_minor(minor, right, land_minor_right, send, recv, slot)
    slot += minor - 1
    begin_factor(
        dot(total[0], total[0], 1, 1, highest) + dot(total[1], total[1], 1, 1, highest), work
    )
    pairs = rank // 2
    marks = [0, pairs * 5 // 16, pairs // 2, pairs * 11 // 16, pairs]
    eliminate(work, marks[0], marks[1])
    arrive(copies)
    value = right[rows_at(q, n_quarter), :]
    for j in range(minor - 1):
        value = value + land_minor_right[j]
    quarter_right[...] = value
    copies = scatter_major(minor, major, quarter_right, land_major_right, send, recv, slot)
    slot += major - 1
    eliminate(work, marks[1], marks[2])
    arrive(copies)
    value = quarter_right[rows_at(z, n_own), :]
    for j in range(major - 1):
        value = value + land_major_right[j]
    own = rows_at(q * major + z, n_own)
    total_right[own, :] = value
    copies = gather(minor, major, True, total_right, own, send, recv, slot)
    slot += major - 1
    eliminate(work, marks[2], marks[3])
    arrive(copies)
    copies = gather(minor, major, False, total_right, rows_at(q, n_quarter), send, recv, slot)
    eliminate(work, marks[3], marks[4])
    inverse[...] = finish_factor(work)
    for h, (start, size) in enumerate(spans):
        ortho[start:start + size, :] = dot(
            total[h, :, :size], inverse[...], 0, 1, highest
        )
    arrive(copies)
    new_basis[...] = dot(inverse[...], total_right[...], 1, 0, highest) * (
        1.0 / (minor * major)
    )
    store.wait()


def factors(minor, major, activations, out_grads, error_state, basis):
    tokens, rows = activations.shape
    columns, rank = basis.shape
    width = -(-rows // 256) * 128
    n_quarter = rank // minor
    n_own = n_quarter // major
    copies = 2 + 4 * (minor - 1) + 4 * (major - 1)
    near = pl.BlockSpec(memory_space=pltpu.VMEM)
    far = pl.BlockSpec(memory_space=pl.ANY)
    f32, bf16 = jnp.float32, jnp.bfloat16
    return pl.pallas_call(
        functools.partial(factor_kernel, minor, major),
        out_shape=(
            jax.ShapeDtypeStruct((rows, columns), f32),
            jax.ShapeDtypeStruct((rows, rank), f32),
            jax.ShapeDtypeStruct((rank, columns), f32),
        ),
        in_specs=[far, far, far, near],
        out_specs=(far, near, near),
        scratch_shapes=[
            pltpu.VMEM((tokens, rows), bf16),
            pltpu.VMEM((tokens, columns), bf16),
            pltpu.VMEM((rows, columns), bf16),
            pltpu.VMEM((rows, columns), f32),
            pltpu.VMEM((rows, columns), bf16),
            pltpu.VMEM((rows, columns), bf16),
            pltpu.VMEM((2, rank, width), f32),
            pltpu.VMEM((rank, width), f32),
            pltpu.VMEM((rank, width), f32),
            pltpu.VMEM((n_quarter, width), f32),
            pltpu.VMEM((minor - 1, n_quarter, width), f32),
            pltpu.VMEM((major - 1, n_own, width), f32),
            pltpu.VMEM((2, rank, width), f32),
            pltpu.VMEM((rank, columns), f32),
            pltpu.VMEM((n_quarter, columns), f32),
            pltpu.VMEM((minor - 1, n_quarter, columns), f32),
            pltpu.VMEM((major - 1, n_own, columns), f32),
            pltpu.VMEM((rank, columns), f32),
            pltpu.VMEM((rank, rank), f32),
            pltpu.VMEM((rank, rank), f32),
            pltpu.SemaphoreType.DMA((copies,)),
            pltpu.SemaphoreType.DMA((copies,)),
            pltpu.SemaphoreType.DMA((4,)),
        ],
        compiler_params=pltpu.CompilerParams(
            collective_id=0, has_side_effects=True, vmem_limit_bytes=58 * 1024 * 1024
        ),
    )(activations, out_grads, error_state, basis)


def pushed(minor, major, activations, out_grads, error_state, basis, master, first_moment,
           second_moment):
    merged, orthonormal, basis_rows = factors(
        minor, major, activations, out_grads, error_state, basis
    )
    decompressed = jnp.dot(orthonormal, basis_rows, precision=high)
    new_error = (merged - decompressed).astype(jnp.bfloat16)
    rows_dev = master.shape[0]
    row_offset = lax.axis_index("dp") * rows_dev
    update = jnp.dot(
        lax.dynamic_slice_in_dim(orthonormal, row_offset, rows_dev, 0), basis_rows, precision=high
    )
    new_first, new_second, new_master = adam(update, master, first_moment, second_moment)
    new_params = lax.all_gather(new_master.astype(jnp.bfloat16), "shard", axis=1, tiled=True)
    return (new_params, new_error, update, new_first, new_second, new_master, basis_rows.T)


def summed_by_psum(activations, out_grads, error_state, basis, master, first_moment,
                   second_moment):
    product = lax.dot_general(
        activations, out_grads, (((0,), (0,)), ((), ())), preferred_element_type=jnp.float32
    )
    merged = product + error_state.astype(jnp.float32)
    rows_dev = master.shape[0]
    partial_value = jnp.dot(merged, basis, precision=highest)
    summed = lax.psum(partial_value, ("dp", "shard"))
    gram_matrix = jnp.dot(summed.T, summed, precision=highest)
    orthonormal = solve_rows(gram_matrix, summed)
    local_right = lax.dot_general(merged, orthonormal, (((0,), (0,)), ((), ())), precision=highest)
    new_basis = lax.psum(local_right, "dp") / lax.axis_size("dp")
    decompressed = lax.dot_general(
        orthonormal, new_basis, (((1,), (1,)), ((), ())), precision=highest
    )
    new_error = (merged - decompressed).astype(jnp.bfloat16)
    row_offset = lax.axis_index("dp") * rows_dev
    update = lax.dynamic_slice_in_dim(decompressed, row_offset, rows_dev, 0)
    new_first, new_second, new_master = adam(update, master, first_moment, second_moment)
    new_params = lax.all_gather(new_master.astype(jnp.bfloat16), "shard", axis=1, tiled=True)
    return (new_params, new_error, update, new_first, new_second, new_master, new_basis)


def solution(mesh):
    replicas, shards = mesh.shape["dp"], mesh.shape["shard"]
    minor = 1
    while minor * minor < replicas:
        minor *= 2
    major = replicas // minor
    placed = (
        P("dp", None),
        P("dp", "shard"),
        P("dp", "shard"),
        P("shard", None),
        P("dp", "shard"),
        P("dp", "shard"),
        P("dp", "shard"),
    )

    def step(activations, out_grads, error_state, basis, master, first_moment, second_moment):
        if shards == 2 and minor * major == replicas and basis.shape[1] % (8 * replicas) == 0:
            body = functools.partial(pushed, minor, major)
        else:
            body = summed_by_psum
        return jax.shard_map(
            body,
            mesh=mesh,
            in_specs=placed,
            out_specs=(
                P("dp", None),
                P("dp", "shard"),
                P("dp", "shard"),
                P("dp", "shard"),
                P("dp", "shard"),
                P("dp", "shard"),
                P("shard", None),
            ),
            check_vma=False,
        )(activations, out_grads, error_state, basis, master, first_moment, second_moment)

    return step
```

```python
import functools

import jax
import jax.numpy as jnp
from jax import lax
from jax.experimental import pallas as pl
from jax.experimental.pallas import tpu as pltpu
from jax.sharding import PartitionSpec as P

beta_one = 0.9
beta_two = 0.95
step_size = 0.001
adam_epsilon = 1e-08
ridge_scale = 1e-06
highest = lax.Precision.HIGHEST
high = lax.Precision.HIGH
MESH = pl.DeviceIdType.MESH


def solve_rows(gram_matrix, row_piece):
    width = gram_matrix.shape[0]
    ridge_term = (
        ridge_scale * jnp.trace(gram_matrix) / width * jnp.eye(width, dtype=gram_matrix.dtype)
    )
    factor = jnp.linalg.cholesky(gram_matrix + ridge_term)
    return jax.scipy.linalg.solve_triangular(factor, row_piece.T, lower=True).T


def adam(update, master, first_moment, second_moment):
    new_first = beta_one * first_moment + (1.0 - beta_one) * update
    new_second = beta_two * second_moment + (1.0 - beta_two) * update * update
    new_master = master - step_size * new_first / (jnp.sqrt(new_second) + adam_epsilon)
    return new_first, new_second, new_master


def rows_at(index, size):
    return pl.ds(pl.multiple_of(index * size, size), size)


def greet(minor, major, pair):
    dp, core = lax.axis_index("dp"), lax.axis_index("shard")
    q, z = lax.rem(dp, minor), lax.div(dp, minor)
    barrier = pltpu.get_barrier_semaphore()
    count = 0
    if pair:
        pl.semaphore_signal(
            barrier, inc=1, device_id={"dp": dp, "shard": 1 - core}, device_id_type=MESH
        )
        count += 1
    for j in range(1, minor):
        peer = z * minor + lax.rem(q + j, minor)
        pl.semaphore_signal(
            barrier, inc=1, device_id={"dp": peer, "shard": core}, device_id_type=MESH
        )
        count += 1
    for j in range(1, major):
        peer = lax.rem(z + j, major) * minor + q
        pl.semaphore_signal(
            barrier, inc=1, device_id={"dp": peer, "shard": core}, device_id_type=MESH
        )
        count += 1
    pl.semaphore_wait(barrier, count)


def push(src, dst, send, recv, slot, dp, core):
    copy = pltpu.make_async_remote_copy(
        src_ref=src,
        dst_ref=dst,
        send_sem=send.at[slot],
        recv_sem=recv.at[slot],
        device_id={"dp": dp, "shard": core},
        device_id_type=MESH,
    )
    copy.start()
    return copy


def scatter_minor(minor, source, land, send, recv, slot):
    dp, core = lax.axis_index("dp"), lax.axis_index("shard")
    q, z = lax.rem(dp, minor), lax.div(dp, minor)
    size = source.shape[0] // minor
    copies = []
    for j in range(1, minor):
        to = lax.rem(q + j, minor)
        copies.append(
            push(source.at[rows_at(to, size)], land.at[j - 1], send, recv, slot + j - 1,
                 z * minor + to, core)
        )
    return copies


def scatter_major(minor, major, source, land, send, recv, slot):
    dp, core = lax.axis_index("dp"), lax.axis_index("shard")
    q, z = lax.rem(dp, minor), lax.div(dp, minor)
    size = source.shape[0] // major
    copies = []
    for j in range(1, major):
        to = lax.rem(z + j, major)
        copies.append(
            push(source.at[rows_at(to, size)], land.at[j - 1], send, recv, slot + j - 1,
                 to * minor + q, core)
        )
    return copies


def gather(minor, major, along_major, ref, rows, send, recv, slot):
    dp, core = lax.axis_index("dp"), lax.axis_index("shard")
    q, z = lax.rem(dp, minor), lax.div(dp, minor)
    copies = []
    for j in range(1, major if along_major else minor):
        if along_major:
            peer = lax.rem(z + j, major) * minor + q
        else:
            peer = z * minor + lax.rem(q + j, minor)
        copies.append(push(ref.at[rows], ref.at[rows], send, recv, slot + j - 1, peer, core))
    return copies


def arrive(copies):
    for copy in copies:
        copy.wait()


def halves(value):
    top = value.astype(jnp.bfloat16)
    rest = (value - top.astype(jnp.float32)).astype(jnp.bfloat16)
    return jnp.concatenate([top, rest], axis=0)


def fold(value):
    rank = value.shape[0] // 2
    return value[:rank] + value[rank:]


def dot(left, right, left_dim, right_dim, precision=None):
    return lax.dot_general(
        left, right, (((left_dim,), (right_dim,)), ((), ())), precision=precision,
        preferred_element_type=jnp.float32,
    )


def begin_factor(gram, work):
    rank = gram.shape[0]
    lane = lax.broadcasted_iota(jnp.int32, (rank, rank), 1)
    line = lax.broadcasted_iota(jnp.int32, (rank, rank), 0)
    trace = jnp.sum(jnp.where(lane == line, gram, 0.0), keepdims=True)
    work[...] = gram + jnp.where(lane == line, ridge_scale * trace / rank, 0.0)


def eliminate(work, first, last):
    rank = work.shape[0]
    lane = lax.broadcasted_iota(jnp.int32, (rank, rank), 1)
    line = lax.broadcasted_iota(jnp.int32, (rank, rank), 0)
    lane_row, line_column = lane[:1], line[:, :1]

    def pick(value, index, places):
        return jnp.sum(jnp.where(places == index, value, 0.0), axis=1, keepdims=True)

    def step(pair, carry):
        j = 2 * pair
        k = j + 1
        matrix = work[...]
        row_j, row_k = work[pl.ds(j, 1), :], work[pl.ds(k, 1), :]
        column_j, column_k = pick(matrix, j, lane), pick(matrix, k, lane)
        jj, jk = pick(row_j, j, lane_row), pick(row_j, k, lane_row)
        kj, kk = pick(row_k, j, lane_row), pick(row_k, k, lane_row)
        inverse_j = 1.0 / jj
        ratio = kj * inverse_j
        inverse_k = 1.0 / (kk - ratio * jk)
        scale_j = jnp.where(line_column > j, column_j * inverse_j, 0.0)
        scale_k = jnp.where(line_column > k, (column_k - scale_j * jk) * inverse_k, 0.0)
        unit_j = jnp.where(lane_row == j, 1.0, row_j)
        unit_k = jnp.where(
            lane_row == k, 1.0, jnp.where(lane_row == j, 0.0, row_k) - ratio * unit_j
        )
        matrix = jnp.where((lane == j) & (line > j), 0.0, matrix) - scale_j * unit_j
        matrix = jnp.where((lane == k) & (line > k), 0.0, matrix) - scale_k * unit_k
        work[...] = matrix
        return carry

    lax.fori_loop(first, last, step, 0)


def finish_factor(work):
    rank = work.shape[0]
    lane = lax.broadcasted_iota(jnp.int32, (rank, rank), 1)
    line = lax.broadcasted_iota(jnp.int32, (rank, rank), 0)
    value = work[...]
    pivots = jnp.sum(jnp.where(lane == line, value, 0.0), axis=1, keepdims=True)
    unit = jnp.where(lane == line, 1.0, jnp.where(lane < line, value, 0.0))
    return unit * lax.rsqrt(pivots)


def factor_kernel(minor, major, a_far, b_far, e_far, basis, error_far, ortho, new_basis,
                  a, b, e, merged, merged_top, merged_rest,
                  part, half, land_core, quarter, land_minor, land_major, total,
                  right, quarter_right, land_minor_right, land_major_right, total_right,
                  work, inverse, send, recv, local):
    dp, core = lax.axis_index("dp"), lax.axis_index("shard")
    q, z = lax.rem(dp, minor), lax.div(dp, minor)
    loads = [
        pltpu.make_async_copy(far, near, local.at[i])
        for i, (far, near) in enumerate(((b_far, b), (a_far, a), (e_far, e)))
    ]
    for load in loads:
        load.start()
    greet(minor, major, True)

    rows, columns = merged.shape
    count = half.shape[0]
    piece = half.shape[2]
    width = count * piece
    spans = [(0, width), (width, rows - width)]
    merged_top[rows:, :] = jnp.zeros_like(merged_top[rows:, :])
    merged_rest[rows:, :] = jnp.zeros_like(merged_rest[rows:, :])
    basis_parts = halves(basis[...].T)
    loads[0].wait()
    token_parts = halves(fold(dot(basis_parts, b[...], 1, 0)))
    loads[1].wait()
    loads[2].wait()
    for h, (start, size) in enumerate(spans):
        value = fold(
            dot(token_parts, a[start:start + size, :], 1, 1)
            + dot(basis_parts, e[start:start + size, :], 1, 1)
        )
        for k in range(count):
            held = min(piece, size - k * piece)
            if held < piece:
                part[h, k] = jnp.zeros(part.shape[2:], jnp.float32)
            part[h, k, :, :held] = value[:, k * piece:k * piece + held]

    def keep(place, value):
        merged[place, :] = value
        top = value.astype(jnp.bfloat16)
        merged_top[place, :] = top
        merged_rest[place, :] = (value - top.astype(jnp.float32)).astype(jnp.bfloat16)

    def tile(i, carry):
        place = rows_at(i, 256)
        keep(place, dot(a[place, :], b[...], 1, 1) + e[place, :].astype(jnp.float32))
        return carry

    full = rows // 256
    cuts = [min(cut, full) for cut in (0, 2, 3, 4)] + [full]

    def tiles(stage):
        if cuts[stage] < cuts[stage + 1]:
            lax.fori_loop(cuts[stage], cuts[stage + 1], tile, 0)

    slots = iter(range(send.shape[0]))

    def take(number):
        return [next(slots) for unused in range(number)][0]

    def all_sum(source, begin, land_one, middle, land_two, result, between):
        n_quarter = middle.shape[1]
        n_own = n_quarter // major
        moving = []
        for k in range(count):
            begin(k)
            moving.append(
                scatter_minor(minor, source.at[k], land_one.at[k], send, recv, take(minor - 1))
            )
        between(0)
        for k in range(count):
            arrive(moving[k])
            value = source[k, rows_at(q, n_quarter), :]
            for j in range(minor - 1):
                value = value + land_one[k, j]
            middle[k] = value
            moving[k] = scatter_major(
                minor, major, middle.at[k], land_two.at[k], send, recv, take(major - 1)
            )
        between(1)
        own = rows_at(q * major + z, n_own)
        for k in range(count):
            arrive(moving[k])
            value = middle[k, rows_at(z, n_own), :]
            for j in range(major - 1):
                value = value + land_two[k, j]
            result(k)[own, :] = value
            moving[k] = gather(minor, major, True, result(k), own, send, recv, take(major - 1))
        between(2)
        own = rows_at(q, n_quarter)
        for k in range(count):
            arrive(moving[k])
            moving[k] = gather(minor, major, False, result(k), own, send, recv, take(minor - 1))
        between(3)
        return moving

    crossing = [
        push(part.at[1 - core, k], land_core.at[k], send, recv, take(1), dp, 1 - core)
        for k in range(count)
    ]

    def begin_left(k):
        arrive([crossing[k]])
        half[k] = part[core, k] + land_core[k]

    moving = all_sum(
        half, begin_left, land_minor, quarter, land_major, lambda k: total.at[core, k], tiles
    )
    crossing = []
    for k in range(count):
        arrive(moving[k])
        mine = total.at[core, k]
        crossing.append(push(mine, mine, send, recv, take(1), dp, 1 - core))
    if full * 256 < rows:
        place = slice(full * 256, rows)
        keep(place, dot(a[place, :], b[...], 1, 1) + e[place, :].astype(jnp.float32))

    rank = work.shape[0]
    across = right.shape[2]
    bands = [(k * across, min(across, columns - k * across)) for k in range(count)]

    def joined(h):
        return jnp.concatenate([total[h, k] for k in range(count)], axis=1)

    def product(parts, place, start, size):
        return fold(dot(parts, merged_top[place, start:start + size], 1, 0)) + dot(
            parts[:rank], merged_rest[place, start:start + size], 1, 0
        )

    parts = halves(joined(core))
    for k, (start, size) in enumerate(bands):
        if size < across:
            right[k] = jnp.zeros(right.shape[1:], jnp.float32)
        right[k, :, :size] = product(parts, rows_at(core, width), start, size)
    arrive(crossing)
    parts = halves(joined(1 - core))

    def begin_right(k):
        start, size = bands[k]
        right[k, :, :size] += product(parts, rows_at(1 - core, width), start, size)

    pairs = rank // 2
    marks = [0, pairs * 3 // 16, pairs * 5 // 16, pairs * 7 // 16, pairs]

    def factor(stage):
        if stage == 0:
            first, second = joined(0), joined(1)
            begin_factor(
                dot(first, first, 1, 1, highest) + dot(second, second, 1, 1, highest), work
            )
        eliminate(work, marks[stage], marks[stage + 1])

    moving = all_sum(
        right, begin_right, land_minor_right, quarter_right, land_major_right,
        lambda k: total_right.at[k], factor,
    )
    inverse[...] = finish_factor(work)
    for h, (start, size) in enumerate(spans):
        ortho[start:start + size, :] = dot(joined(h), inverse[...], 0, 1, highest)[:size]
    for k, (start, size) in enumerate(bands):
        arrive(moving[k])
        new_basis[:, start:start + size] = dot(
            inverse[...], total_right[k], 1, 0, highest
        )[:, :size] * (1.0 / (minor * major))
    value = new_basis[...]
    top = value.astype(jnp.bfloat16)
    rest = (value - top.astype(jnp.float32)).astype(jnp.bfloat16)
    basis_stack = jnp.concatenate([top, rest, top], axis=0)
    stores = []
    step_rows = -(-rows // 64) * 16
    for i, start in enumerate(range(0, rows, step_rows)):
        place = slice(start, min(start + step_rows, rows))
        value = ortho[place, :]
        top = value.astype(jnp.bfloat16)
        rest = (value - top.astype(jnp.float32)).astype(jnp.bfloat16)
        stack = jnp.concatenate([top, top, rest], axis=1)
        e[place, :] = (merged[place, :] - dot(stack, basis_stack, 1, 0)).astype(jnp.bfloat16)
        store = pltpu.make_async_copy(e.at[place], error_far.at[place], local.at[3 + i])
        store.start()
        stores.append(store)
    for store in stores:
        store.wait()


def factors(minor, major, activations, out_grads, error_state, basis):
    tokens, rows = activations.shape
    columns, rank = basis.shape
    width = -(-rows // 256) * 128
    n_quarter = rank // minor
    n_own = n_quarter // major
    count = 2 if width % 256 == 0 else 1
    piece = width // count
    across = -(-columns // (128 * count)) * 128
    copies = count * (2 + 4 * (minor - 1) + 4 * (major - 1))
    near = pl.BlockSpec(memory_space=pltpu.VMEM)
    far = pl.BlockSpec(memory_space=pl.ANY)
    f32, bf16 = jnp.float32, jnp.bfloat16
    return pl.pallas_call(
        functools.partial(factor_kernel, minor, major),
        out_shape=(
            jax.ShapeDtypeStruct((rows, columns), bf16),
            jax.ShapeDtypeStruct((rows, rank), f32),
            jax.ShapeDtypeStruct((rank, columns), f32),
        ),
        in_specs=[far, far, far, near],
        out_specs=(far, near, near),
        scratch_shapes=[
            pltpu.VMEM((rows, tokens), bf16),
            pltpu.VMEM((columns, tokens), bf16),
            pltpu.VMEM((rows, columns), bf16),
            pltpu.VMEM((rows, columns), f32),
            pltpu.VMEM((2 * width, columns), bf16),
            pltpu.VMEM((2 * width, columns), bf16),
            pltpu.VMEM((2, count, rank, piece), f32),
            pltpu.VMEM((count, rank, piece), f32),
            pltpu.VMEM((count, rank, piece), f32),
            pltpu.VMEM((count, n_quarter, piece), f32),
            pltpu.VMEM((count, minor - 1, n_quarter, piece), f32),
            pltpu.VMEM((count, major - 1, n_own, piece), f32),
            pltpu.VMEM((2, count, rank, piece), f32),
            pltpu.VMEM((count, rank, across), f32),
            pltpu.VMEM((count, n_quarter, across), f32),
            pltpu.VMEM((count, minor - 1, n_quarter, across), f32),
            pltpu.VMEM((count, major - 1, n_own, across), f32),
            pltpu.VMEM((count, rank, across), f32),
            pltpu.VMEM((rank, rank), f32),
            pltpu.VMEM((rank, rank), f32),
            pltpu.SemaphoreType.DMA((copies,)),
            pltpu.SemaphoreType.DMA((copies,)),
            pltpu.SemaphoreType.DMA((7,)),
        ],
        compiler_params=pltpu.CompilerParams(
            collective_id=0, has_side_effects=True, vmem_limit_bytes=58 * 1024 * 1024
        ),
    )(activations.T, out_grads.T, error_state, basis)


def pushed(minor, major, activations, out_grads, error_state, basis, master, first_moment,
           second_moment):
    new_error, orthonormal, basis_rows = factors(
        minor, major, activations, out_grads, error_state, basis
    )
    rows_dev = master.shape[0]
    row_offset = lax.axis_index("dp") * rows_dev
    update = jnp.dot(
        lax.dynamic_slice_in_dim(orthonormal, row_offset, rows_dev, 0), basis_rows, precision=high
    )
    new_first, new_second, new_master = adam(update, master, first_moment, second_moment)
    new_params = lax.all_gather(new_master.astype(jnp.bfloat16), "shard", axis=1, tiled=True)
    return (new_params, new_error, update, new_first, new_second, new_master, basis_rows.T)


def summed_by_psum(activations, out_grads, error_state, basis, master, first_moment,
                   second_moment):
    product = lax.dot_general(
        activations, out_grads, (((0,), (0,)), ((), ())), preferred_element_type=jnp.float32
    )
    merged = product + error_state.astype(jnp.float32)
    rows_dev = master.shape[0]
    partial_value = jnp.dot(merged, basis, precision=highest)
    summed = lax.psum(partial_value, ("dp", "shard"))
    gram_matrix = jnp.dot(summed.T, summed, precision=highest)
    orthonormal = solve_rows(gram_matrix, summed)
    local_right = lax.dot_general(merged, orthonormal, (((0,), (0,)), ((), ())), precision=highest)
    new_basis = lax.psum(local_right, "dp") / lax.axis_size("dp")
    decompressed = lax.dot_general(
        orthonormal, new_basis, (((1,), (1,)), ((), ())), precision=highest
    )
    new_error = (merged - decompressed).astype(jnp.bfloat16)
    row_offset = lax.axis_index("dp") * rows_dev
    update = lax.dynamic_slice_in_dim(decompressed, row_offset, rows_dev, 0)
    new_first, new_second, new_master = adam(update, master, first_moment, second_moment)
    new_params = lax.all_gather(new_master.astype(jnp.bfloat16), "shard", axis=1, tiled=True)
    return (new_params, new_error, update, new_first, new_second, new_master, new_basis)


def solution(mesh):
    replicas, shards = mesh.shape["dp"], mesh.shape["shard"]
    minor = 1
    while minor * minor < replicas:
        minor *= 2
    major = replicas // minor
    placed = (
        P("dp", None),
        P("dp", "shard"),
        P("dp", "shard"),
        P("shard", None),
        P("dp", "shard"),
        P("dp", "shard"),
        P("dp", "shard"),
    )

    def step(activations, out_grads, error_state, basis, master, first_moment, second_moment):
        if shards == 2 and minor * major == replicas and basis.shape[1] % (8 * replicas) == 0:
            body = functools.partial(pushed, minor, major)
        else:
            body = summed_by_psum
        return jax.shard_map(
            body,
            mesh=mesh,
            in_specs=placed,
            out_specs=(
                P("dp", None),
                P("dp", "shard"),
                P("dp", "shard"),
                P("dp", "shard"),
                P("dp", "shard"),
                P("dp", "shard"),
                P("shard", None),
            ),
            check_vma=False,
        )(activations, out_grads, error_state, basis, master, first_moment, second_moment)

    return step
```
